32 devices in a mesh: grp: 2 (over y), row: 4 (over z), col: 2 (over x), sub: 2 (over core).
Axes of the slice: x: 2, y: 2, z: 4, core: 2. Of those that a mesh axis runs over, the one named last changes fastest.
Arguments:
- features: bfloat16 [5120, 64], P(('grp', 'row', 'col', 'sub')), parts along dimension 0, may hold values from -6 to 6
- probes: bfloat16 [5120, 33], P(('grp', 'row', 'col', 'sub')), parts along dimension 0, may hold values from -6 to 6
- tile_live: int32 [10], P('grp'), parts along dimension 0, may hold values from 1 to 512, 1920 in all
- lengthscale: float32 [2], P('grp'), parts along dimension 0, may hold values from 3 to 5
Outputs:
- kernel_product: float32 [5120, 33], P(('grp', 'row', 'col', 'sub')), parts along dimension 0
- derivative_product: float32 [5120, 33], P(('grp', 'row', 'col', 'sub')), parts along dimension 0
The draws below stay inside these ranges and needn't reach their ends.
There are 2 independent parts, one for each index of `grp`. The reference program is written for one: setup_inputs(seed, part) draws one part's arguments, and reference() takes and returns one part's arrays. A program takes and returns all parts, laid end to end along the dimension named above; each array names one. Nothing has to cross between parts.
Inputs may be any that keep to these rules, and one draw needn't show every extreme that they name: Tile t holds evaluated designs in its first tile_live[t] slots; the counts sum to 1920 and at least one tile is full.
All inputs are finite; a program needn't handle non-finite values.
Results may differ from the reference program's by a relative error of at most 0.0003.
Values may be sent and summed in bfloat16 or wider, within the bound.
A program may use at most 64 MiB of HBM per device.

```python
import math
import jax
import jax.numpy as jnp
import numpy as np
from jax import lax

F = 64
C = 33
TILE = 512
N = 2560
NT = 5


def block_scale(key, dims, split, smallest, high):
    def one(position, blocks):
        draws = jax.random.uniform(jax.random.fold_in(jax.random.fold_in(key, 6), position), (blocks,), jnp.float32, smallest / len(split), high / len(split))
        return jnp.repeat(jnp.exp(draws), dims[position] // blocks).reshape((-1,) + (1,) * (len(dims) - position - 1))

    gain = one(*split[0])
    for cut in split[1:]:
        gain = gain * one(*cut)
    return gain


def length_profile(number_of, total, most, lean):
    loads = [(1 << 20) // math.isqrt(grade ** lean) + 1 for grade in range(2, number_of + 1)]
    rest, holding = total - most - (number_of - 1), [1] * (number_of - 1)
    while rest > 0:
        free = [i for i in range(number_of - 1) if holding[i] < most]
        whole, budget = sum([loads[i] for i in free]), rest
        for i in free:
            extra = min(most - holding[i], max(1, budget * loads[i] // whole), rest)
            holding[i] = holding[i] + extra
            rest = rest - extra
    return np.array([most] + holding)


def ragged_sizes(key, count, total, reach, lean):
    if count == 2:
        one = jax.random.randint(key, (), max(1, total - reach), min(reach, total - 1) + 1)
        return jnp.stack([one, total - one])
    tallies = jnp.asarray(length_profile(count, total, reach, lean), jnp.int32)
    twos = (count - 1) // 2
    donor, sink = tallies[1:1 + 2 * twos:2], tallies[2:2 + 2 * twos:2]
    margin = jnp.minimum(donor - 1, reach - sink)
    passed = jax.random.randint(jax.random.fold_in(key, 1), (twos,), 0, 1 << 20) % (margin + 1)
    tallies = tallies.at[1:1 + 2 * twos:2].set(donor - passed).at[2:2 + 2 * twos:2].set(sink + passed)
    return tallies[jax.random.permutation(jax.random.fold_in(key, 2), count)]


def noise(own_key, shape, spread, most, split=(), held_as=jnp.bfloat16):
    values = spread * jax.random.normal(own_key, shape, jnp.float32)
    if split:
        values = values * block_scale(own_key, shape, split, -0.22, 0.18)
    return jnp.clip(values, -most, most).astype(held_as)


def setup_inputs(seed: int = 0, part: int = 0) -> dict:
    seeds = jax.random.split(jax.random.key(seed), 5)
    own_keys = jax.random.split(jax.random.fold_in(seeds[4], part), 5)
    return {
        "features": noise(own_keys[0], (N, F), 1.0, 6.0, ((0, 16),)),
        "probes": noise(own_keys[1], (N, C), 1.0, 6.0, ((0, 16),)),
        "tile_live": ragged_sizes(own_keys[2], NT, NT * TILE * 3 // 4, TILE, 0).astype(jnp.int32),
        "lengthscale": jnp.clip(jnp.exp(jax.random.uniform(own_keys[3], (1,), jnp.float32, math.log(3.0), math.log(5.0))), 3.0, 5.0),
    }


ROOT_FIVE = math.sqrt(5.0)

def tile_terms(left_feat, left_norms, all_feat, all_norms, inv_length):
    cross = jnp.dot(left_feat, all_feat.T, precision=lax.Precision.HIGHEST)
    dist_sq = jnp.maximum(left_norms[:, None] + all_norms[None, :] - 2.0 * cross, 0.0)
    scaled = ROOT_FIVE * inv_length * jnp.sqrt(dist_sq)
    decay = jnp.exp(-scaled)
    kmat = (1.0 + scaled + scaled * scaled / 3.0) * decay
    dmat = scaled * scaled * (1.0 + scaled) * decay * (inv_length / 3.0)
    return (kmat, dmat)

def reference(features, probes, tile_live, lengthscale):
    slots = jnp.arange(N, dtype=jnp.int32)
    live = slots % TILE < tile_live[slots // TILE]
    live_float = live.astype(jnp.float32)
    masked = probes * live.astype(jnp.bfloat16)[:, None]
    masked_float = masked.astype(jnp.float32)
    feat_float = features.astype(jnp.float32)
    norms = lax.optimization_barrier(jnp.sum(feat_float * feat_float, axis=1))
    inv_length = 1.0 / lengthscale[0]
    factor = 4.0 / math.sqrt(N)

    def one_tile(tile_number):
        begin = (tile_number * TILE).astype(jnp.int32)
        left_feat = lax.dynamic_slice_in_dim(feat_float, begin, TILE, 0)
        left_norms = lax.dynamic_slice_in_dim(norms, begin, TILE, 0)
        kmat, dmat = tile_terms(left_feat, left_norms, feat_float, norms, inv_length)
        kern = jnp.dot(kmat, masked_float, precision=lax.Precision.HIGHEST)
        deriv = jnp.dot(dmat, masked_float, precision=lax.Precision.HIGHEST)
        return (kern, deriv)
    kern_tiles, deriv_tiles = lax.map(one_tile, jnp.arange(NT, dtype=jnp.int32))
    kernel_product = kern_tiles.reshape(N, C) * (live_float * factor)[:, None]
    derivative_product = deriv_tiles.reshape(N, C) * (live_float * factor)[:, None]
    return (kernel_product, derivative_product)
```

```python
import functools
import math

import jax
import jax.numpy as jnp
from jax import lax
from jax.experimental import pallas as pl
from jax.experimental.pallas import tpu as pltpu
from jax.sharding import PartitionSpec as P

TILE = 512
LANES = 128
MESH = pl.DeviceIdType.MESH
LN2 = math.log(2.0)
TINY = 1e-30


def partner(index, step, size):
    if size & (size - 1):
        return lax.rem(index + step, size)
    other = index
    bit = 1
    while bit < size:
        if step & bit:
            other = other + bit - 2 * bit * lax.rem(lax.div(index, bit), 2)
        bit *= 2
    return other


def source(index, step, size):
    if size & (size - 1):
        return lax.rem(index - step + size, size)
    return partner(index, step, size)


def kernel(
    sizes,
    live_ref, length_ref, feat_ref, probe_ref,
    kern_ref, deriv_ref,
    flip, left, held,
    z_send, z_recv, x_send, x_recv, s_send, s_recv,
):
    rows, cols, total = sizes
    width, shard = feat_ref.shape
    probes = probe_ref.shape[0]
    tiles = live_ref.shape[0]
    padded = flip.shape[1]
    z, x, s = lax.axis_index("row"), lax.axis_index("col"), lax.axis_index("sub")
    grp = lax.axis_index("grp")
    z_peer = [partner(z, m, rows) for m in range(rows)]
    z_from = [source(z, m, rows) for m in range(rows)]
    x_peer = [partner(x, m, cols) for m in range(cols)]
    x_from = [source(x, m, cols) for m in range(cols)]

    def slot(zz, xx, ss):
        begin = ((zz * cols + xx) * 2 + ss) * shard
        return held.at[pl.ds(pl.multiple_of(begin, 32), shard)]

    barrier = pltpu.get_barrier_semaphore()
    targets = [(grp, z_peer[m], x, s) for m in range(1, rows)]
    targets += [(grp, z, x_peer[m], s) for m in range(1, cols)]
    targets += [(grp, z, x, 1 - s)]
    for target in targets:
        pl.semaphore_signal(barrier, inc=1, device_id=target, device_id_type=MESH)

    first = ((z * cols + x) * 2 + s) * shard
    slots = first + lax.broadcasted_iota(jnp.int32, (1, shard), 1)
    live = jnp.zeros((1, shard), jnp.float32)
    for step in range((shard - 2) // TILE + 2):
        tile = lax.div(first, TILE) + step
        inside = slots - tile * TILE
        count = live_ref[jnp.minimum(tile, tiles - 1)]
        live = jnp.where((inside >= 0) & (inside < TILE) & (inside < count), 1.0, live)
    feat = feat_ref[...].astype(jnp.float32)
    norm = jnp.sum(feat * feat, axis=0, keepdims=True)
    high = norm.astype(jnp.bfloat16).astype(jnp.float32)
    middle = (norm - high).astype(jnp.bfloat16).astype(jnp.float32)
    low = norm - high - middle
    ones = jnp.ones((1, shard), jnp.float32)
    base = width + probes
    flip[...] = jnp.zeros_like(flip)
    flip[:width, :shard] = feat
    flip[width:base, :shard] = probe_ref[...].astype(jnp.float32) * live
    for place, row in enumerate((high, middle, low, ones, ones, ones)):
        flip[base + place : base + place + 1, :shard] = row
    mine = slot(z, x, s)
    mine[...] = flip[...].T[:shard].astype(jnp.bfloat16)

    pl.semaphore_wait(barrier, len(targets))

    started = []

    def send(block, send_sem, recv_sem, target):
        copy = pltpu.make_async_remote_copy(
            src_ref=block, dst_ref=block, send_sem=send_sem, recv_sem=recv_sem,
            device_id=target, device_id_type=MESH,
        )
        copy.start()
        started.append(copy)

    def landed(block, send_sem, recv_sem):
        pltpu.make_async_remote_copy(
            src_ref=block, dst_ref=block, send_sem=send_sem, recv_sem=recv_sem,
            device_id=(grp, z, x, 1 - s), device_id_type=MESH,
        ).wait_recv()

    def send_x(m, block):
        for n in range(1, cols):
            send(block, x_send.at[m, n], x_recv.at[m, n], (grp, z, x_peer[n], s))

    def send_s(m, n, block):
        send(block, s_send.at[m, n], s_recv.at[m, n], (grp, z, x, 1 - s))

    send_x(0, mine)
    for m in range(1, rows):
        send(mine, z_send.at[m], z_recv.at[m], (grp, z_peer[m], x, s))
    send_s(0, 0, mine)

    flip[:width, :shard] = -2.0 * feat
    flip[width:base, :shard] = jnp.zeros((probes, shard), jnp.float32)
    for place, row in enumerate((ones, ones, ones, high, middle, low)):
        flip[base + place : base + place + 1, :shard] = row
    left[...] = flip[...].T[:shard].astype(jnp.bfloat16)

    inv = 1.0 / length_ref[0]
    gain = 5.0 * inv * inv / (LN2 * LN2)
    span = 640 if (cols * 2 * shard) % 640 == 0 else shard

    def chunk(begin, sums):
        block = held[pl.ds(pl.multiple_of(begin, 32), span), :]
        dist = lax.dot_general(
            left[...], block, (((1,), (1,)), ((), ())), preferred_element_type=jnp.float32
        )
        square = jnp.maximum(dist * gain, TINY)
        depth = square * lax.rsqrt(square)
        decay = jnp.exp2(-depth)
        kmat = (1.0 + depth * (LN2 + depth * (LN2 * LN2 / 3.0))) * decay
        dmat = square * decay * (1.0 + LN2 * depth)
        done = []
        for mat, kept in zip((kmat, dmat), sums):
            top = mat.astype(jnp.bfloat16)
            rest = (mat - top.astype(jnp.float32)).astype(jnp.bfloat16)
            done.append(
                kept
                + jnp.dot(top, block, preferred_element_type=jnp.float32)
                + jnp.dot(rest, block, preferred_element_type=jnp.float32)
            )
        return tuple(done)

    def compute(m, sums):
        plane = z_from[m] * (cols * 2 * shard)
        pieces = cols * 2 * shard // span
        if pieces == 1:
            return chunk(plane, sums)
        return lax.fori_loop(0, pieces, lambda p, kept: chunk(plane + p * span, kept), sums)

    empty = jnp.zeros((shard, LANES), jnp.float32)
    sums = (empty, empty)
    for m in range(rows):
        if m + 1 < rows:
            block = slot(z_from[m + 1], x, s)
            landed(block, z_send.at[m + 1], z_recv.at[m + 1])
            send_x(m + 1, block)
            send_s(m + 1, 0, block)
        for n in range(1, cols):
            block = slot(z_from[m], x_from[n], s)
            landed(block, x_send.at[m, n], x_recv.at[m, n])
            send_s(m, n, block)
        for n in range(cols):
            landed(slot(z_from[m], x_from[n], 1 - s), s_send.at[m, n], s_recv.at[m, n])
        sums = compute(m, sums)

    factor = 4.0 / math.sqrt(total)
    for out, kept, scale in zip(
        (kern_ref, deriv_ref), sums, (factor, factor * LN2 * LN2 / 3.0 * inv)
    ):
        whole = jnp.concatenate([kept, jnp.zeros((padded - shard, LANES), jnp.float32)], axis=0)
        out[...] = whole.T[width:base, :shard] * (live * scale)
    for copy in started:
        copy.wait_send()


def solution(mesh):
    rows, cols = mesh.shape["row"], mesh.shape["col"]

    def per_device(features, probes, tile_live, lengthscale):
        shard, width = features.shape
        count = probes.shape[1]
        total = shard * rows * cols * 2
        padded = (shard + LANES - 1) // LANES * LANES
        out = jax.ShapeDtypeStruct((count, shard), jnp.float32)
        vmem, smem = pl.BlockSpec(memory_space=pltpu.VMEM), pl.BlockSpec(memory_space=pltpu.SMEM)
        dma = pltpu.SemaphoreType.DMA
        kern, deriv = pl.pallas_call(
            functools.partial(kernel, (rows, cols, total)),
            out_shape=(out, out),
            in_specs=[smem, smem, vmem, vmem],
            out_specs=(vmem, vmem),
            scratch_shapes=[
                pltpu.VMEM((LANES, padded), jnp.float32),
                pltpu.VMEM((shard, LANES), jnp.bfloat16),
                pltpu.VMEM((total, LANES), jnp.bfloat16),
                dma((rows,)), dma((rows,)),
                dma((rows, cols)), dma((rows, cols)),
                dma((rows, cols)), dma((rows, cols)),
            ],
            compiler_params=pltpu.CompilerParams(
                collective_id=0, has_side_effects=True, vmem_limit_bytes=48 << 20
            ),
        )(tile_live, lengthscale, features.T, probes.T)
        return kern.T, deriv.T

    split = P(("grp", "row", "col", "sub"), None)
    return jax.shard_map(
        per_device,
        mesh=mesh,
        in_specs=(split, split, P("grp"), P("grp")),
        out_specs=(split, split),
        check_vma=False,
    )
```

```python
import functools
import math

import jax
import jax.numpy as jnp
from jax import lax
from jax.experimental import pallas as pl
from jax.experimental.pallas import tpu as pltpu
from jax.sharding import PartitionSpec as P

TILE = 512
LANES = 128
MESH = pl.DeviceIdType.MESH
LN2 = math.log(2.0)
TINY = 1e-30


def partner(index, step, size):
    if size & (size - 1):
        return lax.rem(index + step, size)
    other = index
    bit = 1
    while bit < size:
        if step & bit:
            other = other + bit - 2 * bit * lax.rem(lax.div(index, bit), 2)
        bit *= 2
    return other


def source(index, step, size):
    if size & (size - 1):
        return lax.rem(index - step + size, size)
    return partner(index, step, size)


def kernel(
    sizes,
    live_hbm, length_hbm, feat_hbm, probe_hbm,
    out_ref,
    live_ref, length_ref, feat_ref, probe_ref, load_sem,
    flip, left, held,
    x_send, x_recv, s_send, s_recv,
):
    rows, cols = sizes
    width, shard = feat_ref.shape
    probes = probe_ref.shape[0]
    tiles = live_ref.shape[0]
    padded = flip.shape[1]
    z, x, s = lax.axis_index("row"), lax.axis_index("col"), lax.axis_index("sub")
    grp = lax.axis_index("grp")
    z_peer = [partner(z, m, rows) for m in range(rows)]
    z_from = [source(z, m, rows) for m in range(rows)]
    x_peer = [partner(x, m, cols) for m in range(cols)]
    x_from = [source(x, m, cols) for m in range(cols)]

    def slot(zz, xx, ss):
        begin = ((zz * 2 + ss) * cols + xx) * shard
        return held.at[pl.ds(pl.multiple_of(begin, 32), shard)]

    barrier = pltpu.get_barrier_semaphore()
    steps = [(m, n) for m in reversed(range(rows)) for n in reversed(range(cols)) if m or n]
    targets = [(grp, z_peer[m], x_peer[n], s) for m, n in steps]
    targets += [(grp, z, x, 1 - s)]
    for target in targets:
        pl.semaphore_signal(barrier, inc=1, device_id=target, device_id_type=MESH)
    pairs = ((feat_hbm, feat_ref), (probe_hbm, probe_ref), (live_hbm, live_ref), (length_hbm, length_ref))
    loads = [pltpu.make_async_copy(a, b, load_sem.at[k]) for k, (a, b) in enumerate(pairs)]
    for load in loads:
        load.start()
    flip[...] = jnp.zeros_like(flip)
    for load in loads:
        load.wait()

    first = ((z * cols + x) * 2 + s) * shard
    slots = first + lax.broadcasted_iota(jnp.int32, (1, shard), 1)
    live = jnp.zeros((1, shard), jnp.float32)
    for step in range((shard - 2) // TILE + 2):
        tile = lax.div(first, TILE) + step
        inside = slots - tile * TILE
        count = live_ref[jnp.minimum(tile, tiles - 1)]
        live = jnp.where((inside >= 0) & (inside < TILE) & (inside < count), 1.0, live)
    feat = feat_ref[...].astype(jnp.float32)
    norm = jnp.sum(feat * feat, axis=0, keepdims=True)
    high = norm.astype(jnp.bfloat16).astype(jnp.float32)
    middle = (norm - high).astype(jnp.bfloat16).astype(jnp.float32)
    low = norm - high - middle
    ones = jnp.ones((1, shard), jnp.float32)
    base = width + probes
    flip[:width, :shard] = feat
    flip[width:base, :shard] = probe_ref[...].astype(jnp.float32) * live
    for place, row in enumerate((high, middle, low, ones, ones, ones)):
        flip[base + place : base + place + 1, :shard] = row
    mine = slot(z, x, s)
    mine[...] = flip[...].T[:shard].astype(jnp.bfloat16)

    pl.semaphore_wait(barrier, len(targets))

    started = []

    def send(block, send_sem, recv_sem, target):
        copy = pltpu.make_async_remote_copy(
            src_ref=block, dst_ref=block, send_sem=send_sem, recv_sem=recv_sem,
            device_id=target, device_id_type=MESH,
        )
        copy.start()
        started.append(copy)

    def landed(block, send_sem, recv_sem):
        pltpu.make_async_remote_copy(
            src_ref=block, dst_ref=block, send_sem=send_sem, recv_sem=recv_sem,
            device_id=(grp, z, x, 1 - s), device_id_type=MESH,
        ).wait_recv()

    def send_s(m, n, block):
        send(block, s_send.at[m, n], s_recv.at[m, n], (grp, z, x, 1 - s))

    for m, n in steps:
        send(mine, x_send.at[m, n], x_recv.at[m, n], (grp, z_peer[m], x_peer[n], s))
    send_s(0, 0, mine)

    flip[:width, :shard] = -2.0 * feat
    flip[width:base, :shard] = jnp.zeros((probes, shard), jnp.float32)
    for place, row in enumerate((ones, ones, ones, high, middle, low)):
        flip[base + place : base + place + 1, :shard] = row
    left[...] = flip[...].T[:shard].astype(jnp.bfloat16)

    inv = 1.0 / length_ref[0]
    gain = 5.0 * inv * inv / (LN2 * LN2)
    half = cols * shard
    span = 2 * shard if cols % 2 == 0 else shard

    def chunk(begin, sums):
        block = held[pl.ds(pl.multiple_of(begin, 32), span), :]
        dist = lax.dot_general(
            left[...], block, (((1,), (1,)), ((), ())), preferred_element_type=jnp.float32
        )
        square = jnp.maximum(dist * gain, TINY)
        depth = square * lax.rsqrt(square)
        decay = jnp.exp2(-depth)
        kmat = (1.0 + depth * (LN2 + depth * (LN2 * LN2 / 3.0))) * decay
        dmat = square * decay * (1.0 + LN2 * depth)
        done = []
        for mat, kept in zip((kmat, dmat), sums):
            top = mat.astype(jnp.bfloat16)
            rest = (mat - top.astype(jnp.float32)).astype(jnp.bfloat16)
            done.append(
                kept
                + jnp.dot(top, block, preferred_element_type=jnp.float32)
                + jnp.dot(rest, block, preferred_element_type=jnp.float32)
            )
        return tuple(done)

    def compute(m, ss, sums):
        begin = (z_from[m] * 2 + ss) * half
        pieces = half // span
        if pieces == 1:
            return chunk(begin, sums)
        return lax.fori_loop(0, pieces, lambda p, kept: chunk(begin + p * span, kept), sums)

    def other_half(m, sums):
        for n in range(cols):
            landed(slot(z_from[m], x_from[n], 1 - s), s_send.at[m, n], s_recv.at[m, n])
        return compute(m, 1 - s, sums)

    empty = jnp.zeros((shard, LANES), jnp.float32)
    sums = (empty, empty)
    for m in range(rows):
        for n in range(cols):
            if m or n:
                block = slot(z_from[m], x_from[n], s)
                landed(block, x_send.at[m, n], x_recv.at[m, n])
                send_s(m, n, block)
        if m:
            sums = other_half(m - 1, sums)
        sums = compute(m, s, sums)
    sums = other_half(rows - 1, sums)

    for place, (kept, scale) in enumerate(zip(sums, (1.0, LN2 * LN2 / 3.0 * inv))):
        whole = jnp.concatenate([kept, jnp.zeros((padded - shard, LANES), jnp.float32)], axis=0)
        out_ref[place] = whole.T[width:base, :shard] * (live * scale)
    for copy in started:
        copy.wait_send()


def solution(mesh):
    rows, cols = mesh.shape["row"], mesh.shape["col"]

    def per_device(features, probes, tile_live, lengthscale):
        shard, width = features.shape
        count = probes.shape[1]
        total = shard * rows * cols * 2
        padded = (shard + LANES - 1) // LANES * LANES
        out = jax.ShapeDtypeStruct((2, count, shard), jnp.float32)
        vmem, hbm = pl.BlockSpec(memory_space=pltpu.VMEM), pl.BlockSpec(memory_space=pltpu.HBM)
        dma = pltpu.SemaphoreType.DMA
        both = pl.pallas_call(
            functools.partial(kernel, (rows, cols)),
            out_shape=out,
            in_specs=[hbm] * 4,
            out_specs=vmem,
            scratch_shapes=[
                pltpu.SMEM(tile_live.shape, jnp.int32),
                pltpu.SMEM(lengthscale.shape, jnp.float32),
                pltpu.VMEM((width, shard), jnp.bfloat16),
                pltpu.VMEM((count, shard), jnp.bfloat16),
                dma((4,)),
                pltpu.VMEM((LANES, padded), jnp.float32),
                pltpu.VMEM((shard, LANES), jnp.bfloat16),
                pltpu.VMEM((total, LANES), jnp.bfloat16),
                dma((rows, cols)), dma((rows, cols)),
                dma((rows, cols)), dma((rows, cols)),
            ],
            compiler_params=pltpu.CompilerParams(
                collective_id=0, has_side_effects=True, vmem_limit_bytes=(64 << 20) - (64 << 10)
            ),
        )(tile_live, lengthscale, features.T, probes.T)
        factor = 4.0 / math.sqrt(total)
        return (both[0] * factor).T, (both[1] * factor).T

    split = P(("grp", "row", "col", "sub"), None)
    return jax.shard_map(
        per_device,
        mesh=mesh,
        in_specs=(split, split, P("grp"), P("grp")),
        out_specs=(split, split),
        check_vma=False,
    )
```

```python
import functools
import math

import jax
import jax.numpy as jnp
from jax import lax
from jax.experimental import pallas as pl
from jax.experimental.pallas import tpu as pltpu
from jax.sharding import PartitionSpec as P

TILE = 512
LANES = 128
MESH = pl.DeviceIdType.MESH
LN2 = math.log(2.0)
TINY = 1e-30


def partner(index, step, size):
    if size & (size - 1):
        return lax.rem(index + step, size)
    other = index
    bit = 1
    while bit < size:
        if step & bit:
            other = other + bit - 2 * bit * lax.rem(lax.div(index, bit), 2)
        bit *= 2
    return other


def source(index, step, size):
    if size & (size - 1):
        return lax.rem(index - step + size, size)
    return partner(index, step, size)


def kernel(
    sizes,
    live_hbm, length_hbm, feat_hbm, probe_hbm,
    out_ref,
    live_ref, length_ref, feat_ref, probe_ref, load_sem,
    flip, left, held,
    x_send, x_recv, s_send, s_recv,
):
    rows, cols = sizes
    width, shard = feat_ref.shape
    probes = probe_ref.shape[0]
    tiles = live_ref.shape[0]
    padded = flip.shape[1]
    z, x, s = lax.axis_index("row"), lax.axis_index("col"), lax.axis_index("sub")
    grp = lax.axis_index("grp")
    z_peer = [partner(z, m, rows) for m in range(rows)]
    z_from = [source(z, m, rows) for m in range(rows)]
    x_peer = [partner(x, m, cols) for m in range(cols)]
    x_from = [source(x, m, cols) for m in range(cols)]

    def slot(zz, xx, ss):
        begin = ((zz * 2 + ss) * cols + xx) * shard
        return held.at[pl.ds(pl.multiple_of(begin, 32), shard)]

    barrier = pltpu.get_barrier_semaphore()
    steps = [(m, n) for m in range(rows) for n in range(cols) if m or n]
    targets = [(grp, z_peer[m], x_peer[n], s) for m, n in steps]
    targets += [(grp, z, x, 1 - s)]
    for target in targets:
        pl.semaphore_signal(barrier, inc=1, device_id=target, device_id_type=MESH)
    pairs = ((feat_hbm, feat_ref), (probe_hbm, probe_ref), (live_hbm, live_ref), (length_hbm, length_ref))
    loads = [pltpu.make_async_copy(a, b, load_sem.at[k]) for k, (a, b) in enumerate(pairs)]
    for load in loads:
        load.start()
    flip[...] = jnp.zeros_like(flip)
    for load in loads:
        load.wait()

    first = ((z * cols + x) * 2 + s) * shard
    slots = first + lax.broadcasted_iota(jnp.int32, (1, shard), 1)
    live = jnp.zeros((1, shard), jnp.float32)
    for step in range((shard - 2) // TILE + 2):
        tile = lax.div(first, TILE) + step
        inside = slots - tile * TILE
        count = live_ref[jnp.minimum(tile, tiles - 1)]
        live = jnp.where((inside >= 0) & (inside < TILE) & (inside < count), 1.0, live)
    feat = feat_ref[...].astype(jnp.float32)
    norm = jnp.sum(feat * feat, axis=0, keepdims=True)
    high = norm.astype(jnp.bfloat16).astype(jnp.float32)
    middle = (norm - high).astype(jnp.bfloat16).astype(jnp.float32)
    low = norm - high - middle
    ones = jnp.ones((1, shard), jnp.float32)
    base = width + probes
    flip[:width, :shard] = feat
    flip[width:base, :shard] = probe_ref[...].astype(jnp.float32) * live
    for place, row in enumerate((high, middle, low, ones, ones, ones)):
        flip[base + place : base + place + 1, :shard] = row
    mine = slot(z, x, s)
    mine[...] = flip[...].T[:shard].astype(jnp.bfloat16)

    pl.semaphore_wait(barrier, len(targets))

    started = []

    def send(block, send_sem, recv_sem, target):
        copy = pltpu.make_async_remote_copy(
            src_ref=block, dst_ref=block, send_sem=send_sem, recv_sem=recv_sem,
            device_id=target, device_id_type=MESH,
        )
        copy.start()
        started.append(copy)

    def landed(block, send_sem, recv_sem):
        pltpu.make_async_remote_copy(
            src_ref=block, dst_ref=block, send_sem=send_sem, recv_sem=recv_sem,
            device_id=(grp, z, x, 1 - s), device_id_type=MESH,
        ).wait_recv()

    def send_s(m, n, block):
        send(block, s_send.at[m, n], s_recv.at[m, n], (grp, z, x, 1 - s))

    for m, n in steps:
        send(mine, x_send.at[m, n], x_recv.at[m, n], (grp, z_peer[m], x_peer[n], s))
    send_s(0, 0, mine)

    flip[:width, :shard] = -2.0 * feat
    flip[width:base, :shard] = jnp.zeros((probes, shard), jnp.float32)
    for place, row in enumerate((ones, ones, ones, high, middle, low)):
        flip[base + place : base + place + 1, :shard] = row
    left[...] = flip[...].T[:shard].astype(jnp.bfloat16)

    inv = 1.0 / length_ref[0]
    gain = 5.0 * inv * inv / (LN2 * LN2)
    half = cols * shard
    span = 2 * shard if cols % 2 == 0 else shard

    def chunk(begin, sums):
        block = held[pl.ds(pl.multiple_of(begin, 32), span), :]
        dist = lax.dot_general(
            left[...], block, (((1,), (1,)), ((), ())), preferred_element_type=jnp.float32
        )
        square = jnp.maximum(dist * gain, TINY)
        depth = square * lax.rsqrt(square)
        decay = jnp.exp2(-depth)
        kmat = (1.0 + depth * (LN2 + depth * (LN2 * LN2 / 3.0))) * decay
        dmat = square * decay * (1.0 + LN2 * depth)
        done = []
        for mat, kept in zip((kmat, dmat), sums):
            top = mat.astype(jnp.bfloat16)
            rest = (mat - top.astype(jnp.float32)).astype(jnp.bfloat16)
            done.append(
                kept
                + jnp.dot(top, block, preferred_element_type=jnp.float32)
                + jnp.dot(rest, block, preferred_element_type=jnp.float32)
            )
        return tuple(done)

    def compute(m, ss, sums):
        begin = (z_from[m] * 2 + ss) * half
        pieces = half // span
        if pieces == 1:
            return chunk(begin, sums)
        return lax.fori_loop(0, pieces, lambda p, kept: chunk(begin + p * span, kept), sums)

    def other_half(m, sums):
        for n in range(cols):
            landed(slot(z_from[m], x_from[n], 1 - s), s_send.at[m, n], s_recv.at[m, n])
        return compute(m, 1 - s, sums)

    empty = jnp.zeros((shard, LANES), jnp.float32)
    sums = (empty, empty)
    for m in range(rows):
        for n in range(cols):
            if m or n:
                block = slot(z_from[m], x_from[n], s)
                landed(block, x_send.at[m, n], x_recv.at[m, n])
                send_s(m, n, block)
        if m:
            sums = other_half(m - 1, sums)
        sums = compute(m, s, sums)
    sums = other_half(rows - 1, sums)

    for place, (kept, scale) in enumerate(zip(sums, (1.0, LN2 * LN2 / 3.0 * inv))):
        whole = jnp.concatenate([kept, jnp.zeros((padded - shard, LANES), jnp.float32)], axis=0)
        out_ref[place] = whole.T[width:base, :shard] * (live * scale)
    for copy in started:
        copy.wait_send()


def solution(mesh):
    rows, cols = mesh.shape["row"], mesh.shape["col"]

    def per_device(features, probes, tile_live, lengthscale):
        shard, width = features.shape
        count = probes.shape[1]
        total = shard * rows * cols * 2
        padded = (shard + LANES - 1) // LANES * LANES
        out = jax.ShapeDtypeStruct((2, count, shard), jnp.float32)
        vmem, hbm = pl.BlockSpec(memory_space=pltpu.VMEM), pl.BlockSpec(memory_space=pltpu.HBM)
        dma = pltpu.SemaphoreType.DMA
        both = pl.pallas_call(
            functools.partial(kernel, (rows, cols)),
            out_shape=out,
            in_specs=[hbm] * 4,
            out_specs=vmem,
            scratch_shapes=[
                pltpu.SMEM(tile_live.shape, jnp.int32),
                pltpu.SMEM(lengthscale.shape, jnp.float32),
                pltpu.VMEM((width, shard), jnp.bfloat16),
                pltpu.VMEM((count, shard), jnp.bfloat16),
                dma((4,)),
                pltpu.VMEM((LANES, padded), jnp.float32),
                pltpu.VMEM((shard, LANES), jnp.bfloat16),
                pltpu.VMEM((total, LANES), jnp.bfloat16),
                dma((rows, cols)), dma((rows, cols)),
                dma((rows, cols)), dma((rows, cols)),
            ],
            compiler_params=pltpu.CompilerParams(
                collective_id=0, has_side_effects=True, vmem_limit_bytes=(64 << 20) - (64 << 10)
            ),
        )(tile_live, lengthscale, features.T, probes.T)
        factor = 4.0 / math.sqrt(total)
        return (both[0] * factor).T, (both[1] * factor).T

    split = P(("grp", "row", "col", "sub"), None)
    return jax.shard_map(
        per_device,
        mesh=mesh,
        in_specs=(split, split, P("grp"), P("grp")),
        out_specs=(split, split),
        check_vma=False,
    )
```
